1024 devices in a mesh: phase: 4 (over x_lo), dp: 16 (over x_hi, z), expert: 16 (over y, core).
Axes of the slice: x: 8 (x_hi: 2, x_lo: 4; x = x_hi * 4 + x_lo), y: 8, z: 8, core: 2. Of those that a mesh axis runs over, the one named last changes fastest.
Arguments:
- grad_out: bfloat16 [4, 32768, 5120], P('phase', ('dp', 'expert')), may hold values from -6 to 6
- routes: int32 [4, 32768, 2], P('phase', ('dp', 'expert')), may hold values from 0 to 63, as said below
- gates: float32 [4, 32768, 2], P('phase', ('dp', 'expert')), may hold values from 0.2 to 1
- saved_in: bfloat16 [4, 16, 256, 10240], P('phase', 'dp', None, 'expert'), may hold values from -6 to 6
- saved_pre: bfloat16 [4, 16, 16, 256, 768], P('phase', 'dp', 'expert'), may hold values from -4 to 4, as said below
- w_up: bfloat16 [4, 10240, 768], P('phase', 'expert'), may hold values from -0.078125 to 0.078125
- w_down: bfloat16 [4, 768, 10240], P('phase', None, 'expert'), may hold values from -0.21875 to 0.21875
Outputs:
- grad_in: bfloat16 [4, 32768, 5120], P('phase', ('dp', 'expert'))
- grad_up: bfloat16 [4, 768, 10240], P('phase', 'dp', 'expert')
- grad_down: bfloat16 [4, 768, 10240], P('phase', 'dp', 'expert')
The draws below stay inside these ranges and needn't reach their ends.
Inputs may be any that keep to these rules, and one draw needn't show every extreme that they name: `routes`: the two experts of a token differ. In each aligned block of 128 rows (the tokens of one device) every expert below 2 is named by at least one row and at most 16 rows; within each token group (2048 rows) one expert below 2 is named by exactly 16 rows of every block, and the other experts below 2 by at most one eighth of 16 rows (at least one) of each block. saved_pre[s, g, j] is the same for all j with the same j // 8.
All inputs are finite; a program needn't handle non-finite values.
Results may differ from the reference program's by a relative error of at most 0.024.
Values may be sent and summed in bfloat16 or wider, within the bound.
No kernel may reach another device: no remote copies, remote signals or barrier semaphores. Data moves between devices by JAX's collectives and lax.ppermute only.
A program may use at most 32 MiB of HBM per device.

```python
import jax
import jax.numpy as jnp
from jax import lax

D = 5120
HID = 768
NE_ALL = 64
EXPERTS = 2
TOK_DEV = 128
SPLIT = 8
CAP = 16
TOKENS = 32768
N_PHASE = 4
N_DP = 16
N_EXPERT = 16


def draw_saved_pre(key, part):
    key = jax.random.fold_in(key, 7)
    shape = (N_PHASE, N_DP, EXPERTS, N_EXPERT * CAP, HID)
    base = jnp.clip(1.5 * jax.random.normal(key, shape, jnp.float32), -4.0, 4.0)
    return jnp.repeat(base, SPLIT, axis=2).astype(jnp.bfloat16)


def draw_routes(key, part):
    key = jax.random.fold_in(key, 11)
    keys = jax.random.split(key, 7)
    blocks = N_PHASE * N_DP * N_EXPERT
    outer = NE_ALL - EXPERTS
    hot = jax.random.randint(keys[0], (N_PHASE, N_DP, 1), 0, EXPERTS)
    hot = jnp.broadcast_to(hot, (N_PHASE, N_DP, N_EXPERT)).reshape(blocks)
    lesser = max(CAP // 8, 1)
    counts = jax.random.randint(keys[1], (blocks, EXPERTS), 1, lesser + 1)
    expert_ids = jnp.arange(EXPERTS, dtype=jnp.int32)
    counts = jnp.where(expert_ids[None, :] == hot[:, None], CAP, counts)
    ends = jnp.cumsum(counts, axis=1)
    ranks = jax.vmap(lambda sub: jax.random.permutation(sub, TOK_DEV))(jax.random.split(keys[2], blocks))
    segment = jnp.sum((ranks[:, :, None] >= ends[:, None, :]).astype(jnp.int32), axis=2)
    outside = jax.random.randint(keys[3], (blocks, TOK_DEV), 0, outer)
    first = jnp.where(segment < EXPERTS, segment, EXPERTS + outside)
    offset = jax.random.randint(keys[4], (blocks, TOK_DEV), 1, outer)
    anchor = jnp.where(segment < EXPERTS, jax.random.randint(keys[5], (blocks, TOK_DEV), 0, outer), outside)
    second = EXPERTS + (anchor + offset) % outer
    flip = jax.random.randint(keys[6], (blocks, TOK_DEV), 0, 2)
    pick_a = jnp.where(flip == 1, second, first)
    pick_b = jnp.where(flip == 1, first, second)
    both = jnp.stack([pick_a, pick_b], axis=-1)
    return both.reshape(N_PHASE, N_DP * N_EXPERT * TOK_DEV, 2).astype(jnp.int32)


def levels(own_key, extent, pieces, low, top_value):
    def one(dim, blocks):
        draws = jax.random.uniform(jax.random.fold_in(jax.random.fold_in(own_key, 6), dim), (blocks,), jnp.float32, low / len(pieces), top_value / len(pieces))
        return jnp.repeat(jnp.exp(draws), extent[dim] // blocks).reshape((-1,) + (1,) * (len(extent) - dim - 1))

    gain = one(*pieces[0])
    for cut in pieces[1:]:
        gain = gain * one(*cut)
    return gain


def scatter_about(rng, dims, spread, bound, cuts=(), held_as=jnp.bfloat16):
    entries = spread * jax.random.normal(rng, dims, jnp.float32)
    if cuts:
        entries = entries * levels(rng, dims, cuts, -0.22, 0.18)
    return jnp.clip(entries, -bound, bound).astype(held_as)


def setup_inputs(seed: int = 0) -> dict:
    streams_of = jax.random.split(jax.random.key(seed), 8)
    return {
        "grad_out": scatter_about(streams_of[0], (N_PHASE, TOKENS, D), 1.0, 6.0, ((0, 4), (1, 256))),
        "routes": draw_routes(jax.random.fold_in(streams_of[7], 71), 0),
        "gates": jnp.clip(0.2 + 0.8 * jax.random.uniform(streams_of[2], (N_PHASE, TOKENS, 2), jnp.float32) ** levels(streams_of[2], (N_PHASE, TOKENS, 2), ((0, 4), (1, 256)), -0.2, 0.2), 0.2, 1.0),
        "saved_in": scatter_about(streams_of[3], (N_PHASE, N_DP, N_EXPERT * CAP, EXPERTS * D), 1.0, 6.0, ((0, 4), (1, 16), (3, 16))),
        "saved_pre": draw_saved_pre(jax.random.fold_in(streams_of[7], 71), 0),
        "w_up": scatter_about(streams_of[5], (N_PHASE, EXPERTS * D, HID), D ** -0.5, 0.078125, ((0, 4), (1, 16))),
        "w_down": scatter_about(streams_of[6], (N_PHASE, HID, EXPERTS * D), HID ** -0.5, 0.21875, ((0, 4), (2, 16))),
    }


def gelu_parts(pre):
    value = pre.astype(jnp.float32)
    cdf = 0.5 * (1.0 + lax.erf(value * 0.7071067811865476))
    dens = jnp.exp(-0.5 * value * value) * 0.3989422804014327
    return value * cdf, cdf + value * dens


def reference(grad_out, routes, gates, saved_in, saved_pre, w_up, w_down):
    slots_all = N_EXPERT * CAP
    arrived = []
    up_list = []
    down_list = []
    for section in range(N_PHASE):
        up_total = jnp.zeros((HID, EXPERTS * D), jnp.float32)
        down_total = jnp.zeros((HID, EXPERTS * D), jnp.float32)
        token_grads = []
        for group in range(N_DP):
            first = group * N_EXPERT * TOK_DEV
            grads = grad_out[section, first:first + N_EXPERT * TOK_DEV]
            chosen = routes[section, first:first + N_EXPERT * TOK_DEV].reshape(N_EXPERT, TOK_DEV * 2)
            weights = gates[section, first:first + N_EXPERT * TOK_DEV].reshape(-1)
            onehot = (chosen[:, :, None] == jnp.arange(EXPERTS, dtype=jnp.int32)[None, None, :]).astype(jnp.int32)
            before = jnp.cumsum(onehot, axis=1) - onehot
            slot = jnp.sum(before * onehot, axis=2)
            source = jnp.arange(N_EXPERT, dtype=jnp.int32)[:, None]
            where_to = (chosen * slots_all + source * CAP + slot).reshape(-1).astype(jnp.int32)
            scaled = (weights[:, None] * jnp.repeat(grads.astype(jnp.float32), 2, axis=0)).astype(jnp.bfloat16)
            sent = jnp.zeros((EXPERTS * slots_all, D), jnp.bfloat16).at[where_to].set(scaled, mode="drop")
            back_rows = []
            for expert in range(EXPERTS):
                rows = sent[expert * slots_all:(expert + 1) * slots_all]
                inputs = saved_in[section, group][:, expert * D:(expert + 1) * D]
                pre = saved_pre[section, group, expert * SPLIT]
                upper = w_up[section, expert * D:(expert + 1) * D]
                lower = w_down[section][:, expert * D:(expert + 1) * D]
                act, slope = gelu_parts(pre)
                act = act.astype(jnp.bfloat16)
                partial_value = jnp.dot(rows, lower.T, preferred_element_type=jnp.float32)
                hidden_grad = (partial_value * slope).astype(jnp.bfloat16)
                term_down = lax.optimization_barrier(jnp.dot(act.T, rows, preferred_element_type=jnp.float32).astype(jnp.bfloat16))
                term_up = lax.optimization_barrier(jnp.dot(hidden_grad.T, inputs, preferred_element_type=jnp.float32).astype(jnp.bfloat16))
                down_total = down_total.at[:, expert * D:(expert + 1) * D].add(term_down.astype(jnp.float32))
                up_total = up_total.at[:, expert * D:(expert + 1) * D].add(term_up.astype(jnp.float32))
                back_rows.append(jnp.dot(hidden_grad, upper.T, preferred_element_type=jnp.float32).astype(jnp.bfloat16))
            back = jnp.concatenate(back_rows, axis=0)
            picked = back.at[where_to].get(mode="fill", fill_value=0).astype(jnp.float32).reshape(N_EXPERT * TOK_DEV, 2, D)
            total = grads.astype(jnp.float32) + picked[:, 0] + picked[:, 1]
            token_grads.append(total.astype(jnp.bfloat16))
        arrived.append(jnp.concatenate(token_grads, axis=0))
        up_list.append(up_total.astype(jnp.bfloat16))
        down_list.append(down_total.astype(jnp.bfloat16))
    shifted = arrived[1:] + [jnp.zeros((TOKENS, D), jnp.bfloat16)]
    return jnp.stack(shifted, axis=0), jnp.stack(up_list, axis=0), jnp.stack(down_list, axis=0)
```

```python
import jax
import jax.numpy as jnp
from jax import lax
from jax.sharding import PartitionSpec as P


def gelu_parts(pre):
    value = pre.astype(jnp.float32)
    cdf = 0.5 * (1.0 + lax.erf(value * 0.7071067811865476))
    dens = jnp.exp(-0.5 * value * value) * 0.3989422804014327
    return (value * cdf, cdf + value * dens)


def exchange(x, axis, groups=None):
    return lax.all_to_all(x, axis, 0, 0, tiled=True, axis_index_groups=groups)


def to_previous(x):
    peers = lax.axis_size("phase")
    return lax.ppermute(x, "phase", [(i, i - 1) for i in range(1, peers)])


def slot_targets(chosen, experts, slots_per):
    tokens = chosen.shape[0]
    flat = chosen.reshape(-1)
    onehot = (flat[:, None] == jnp.arange(experts, dtype=jnp.int32)[None, :]).astype(jnp.int32)
    before = jnp.cumsum(onehot, axis=0) - onehot
    slot = jnp.sum(before * onehot, axis=1)
    return (flat * slots_per + slot).reshape(tokens, 2)


def sum_over_groups(term):
    count = lax.axis_size("dp")
    hid, quarter = term.shape
    pieces = exchange(term, "dp").reshape(count, hid // count, quarter)
    return jnp.sum(pieces.astype(jnp.float32), axis=0).astype(jnp.bfloat16)


def body(grad_out, routes, gates, saved_in, saved_pre, w_up, w_down):
    count = lax.axis_size("expert")
    grads = grad_out[0]
    chosen = routes[0]
    weights = gates[0]
    tokens, width = grads.shape
    quarter = w_up.shape[1]
    split = width // quarter
    experts = count // split
    slots_per = saved_in.shape[2] // count
    all_slots = experts * slots_per
    members = [[e * split + q for q in range(split)] for e in range(experts)]
    share = count * slots_per // split

    grads_after = to_previous(grads)
    chosen_after = to_previous(chosen)

    target = slot_targets(chosen, experts, slots_per)
    slot_ids = jnp.arange(all_slots, dtype=jnp.int32)
    hit = [(target[:, k][None, :] == slot_ids[:, None]) for k in range(2)]
    place = (hit[0] | hit[1]).astype(jnp.bfloat16)
    gate = jnp.sum(
        jnp.where(hit[0], weights[:, 0][None, :], 0.0)
        + jnp.where(hit[1], weights[:, 1][None, :], 0.0),
        axis=1,
        keepdims=True,
    )
    picked = jnp.dot(place, grads, preferred_element_type=jnp.float32)
    packed = (gate * picked).astype(jnp.bfloat16)
    outgoing = (
        packed.reshape(experts, slots_per, split, quarter)
        .transpose(0, 2, 1, 3)
        .reshape(count * slots_per, quarter)
    )
    rows = exchange(outgoing, "expert")

    partial_value = lax.dot_general(
        rows, w_down[0], (((1,), (1,)), ((), ())), preferred_element_type=jnp.float32
    ).astype(jnp.bfloat16)
    part = lax.axis_index("expert") % split
    pre = saved_pre[0, 0, 0]
    _, slope = gelu_parts(lax.dynamic_slice_in_dim(pre, part * share, share, 0))
    shares = exchange(partial_value, "expert", members).reshape(split, share, -1)
    own_grad = (jnp.sum(shares.astype(jnp.float32), axis=0) * slope).astype(jnp.bfloat16)
    hidden_grad = lax.all_gather(own_grad, "expert", axis_index_groups=members, tiled=True)

    act = gelu_parts(pre)[0].astype(jnp.bfloat16)
    term_down = lax.dot_general(
        act, rows, (((0,), (0,)), ((), ())), preferred_element_type=jnp.float32
    ).astype(jnp.bfloat16)
    down = sum_over_groups(term_down)

    back = lax.dot_general(
        hidden_grad, w_up[0], (((1,), (1,)), ((), ())), preferred_element_type=jnp.float32
    ).astype(jnp.bfloat16)
    returned = to_previous(exchange(back, "expert"))

    term_up = lax.dot_general(
        hidden_grad, saved_in[0, 0], (((0,), (0,)), ((), ())), preferred_element_type=jnp.float32
    ).astype(jnp.bfloat16)
    up = sum_over_groups(term_up)

    unpacked = (
        returned.reshape(experts, split, slots_per, quarter)
        .transpose(0, 2, 1, 3)
        .reshape(all_slots, width)
    )
    target_after = slot_targets(chosen_after, experts, slots_per)
    hit_after = [target_after[:, k][:, None] == slot_ids[None, :] for k in range(2)]
    place_after = (hit_after[0] | hit_after[1]).astype(jnp.bfloat16)
    total = grads_after.astype(jnp.float32) + jnp.dot(
        place_after, unpacked, preferred_element_type=jnp.float32
    )
    return (total.astype(jnp.bfloat16)[None], up[None], down[None])


def solution(mesh):
    in_specs = (
        P("phase", ("dp", "expert"), None),
        P("phase", ("dp", "expert"), None),
        P("phase", ("dp", "expert"), None),
        P("phase", "dp", None, "expert"),
        P("phase", "dp", "expert", None, None),
        P("phase", "expert", None),
        P("phase", None, "expert"),
    )
    out_specs = (
        P("phase", ("dp", "expert"), None),
        P("phase", "dp", "expert"),
        P("phase", "dp", "expert"),
    )
    return jax.shard_map(body, mesh=mesh, in_specs=in_specs, out_specs=out_specs, check_vma=False)
```

```python
import jax
import jax.numpy as jnp
from jax import lax
from jax.sharding import PartitionSpec as P


def gelu_parts(pre):
    value = pre.astype(jnp.float32)
    cdf = 0.5 * (1.0 + lax.erf(value * 0.7071067811865476))
    dens = jnp.exp(-0.5 * value * value) * 0.3989422804014327
    return (value * cdf, cdf + value * dens)


def exchange(x, axis, groups=None):
    return lax.all_to_all(x, axis, 0, 0, tiled=True, axis_index_groups=groups)


def to_previous(x):
    peers = lax.axis_size("phase")
    return lax.ppermute(x, "phase", [(i, i - 1) for i in range(1, peers)])


def slot_targets(chosen, experts, slots_per):
    tokens = chosen.shape[0]
    flat = chosen.reshape(-1)
    onehot = (flat[:, None] == jnp.arange(experts, dtype=jnp.int32)[None, :]).astype(jnp.int32)
    before = jnp.cumsum(onehot, axis=0) - onehot
    slot = jnp.sum(before * onehot, axis=1)
    return (flat * slots_per + slot).reshape(tokens, 2)


def sum_over_groups(term):
    count = lax.axis_size("dp")
    hid, quarter = term.shape
    pieces = exchange(term, "dp").reshape(count, hid // count, quarter)
    return jnp.sum(pieces.astype(jnp.float32), axis=0).astype(jnp.bfloat16)


def scatter_over_groups(term):
    count = lax.axis_size("dp")
    near = count // 2
    hid, quarter = term.shape
    piece = hid // count
    groups = [[h * near + z for z in range(near)] for h in range(2)]
    ordered = term.reshape(2, near, piece, quarter).transpose(1, 0, 2, 3).reshape(hid, quarter)
    summed = lax.psum_scatter(
        ordered, "dp", scatter_dimension=0, axis_index_groups=groups, tiled=True
    )
    return summed.reshape(2, piece, quarter)


def finish_groups(summed):
    count = lax.axis_size("dp")
    near = count // 2
    half = lax.axis_index("dp") // near
    away = lax.dynamic_index_in_dim(summed, 1 - half, 0, keepdims=False)
    keep = lax.dynamic_index_in_dim(summed, half, 0, keepdims=False)
    got = lax.ppermute(away, "dp", [(i, (i + near) % count) for i in range(count)])
    return (keep.astype(jnp.float32) + got.astype(jnp.float32)).astype(jnp.bfloat16)


def body(grad_out, routes, gates, saved_in, saved_pre, w_up, w_down):
    count = lax.axis_size("expert")
    grads = grad_out[0]
    chosen = routes[0]
    weights = gates[0]
    tokens, width = grads.shape
    quarter = w_up.shape[1]
    split = width // quarter
    experts = count // split
    slots_per = saved_in.shape[2] // count
    all_slots = experts * slots_per
    members = [[e * split + q for q in range(split)] for e in range(experts)]
    share = count * slots_per // split
    half = tokens // 2

    target = slot_targets(chosen, experts, slots_per)
    slot_ids = jnp.arange(all_slots, dtype=jnp.int32)
    hit = [(target[:, k][None, :] == slot_ids[:, None]) for k in range(2)]
    place = (hit[0] | hit[1]).astype(jnp.bfloat16)
    gate = jnp.sum(
        jnp.where(hit[0], weights[:, 0][None, :], 0.0)
        + jnp.where(hit[1], weights[:, 1][None, :], 0.0),
        axis=1,
        keepdims=True,
    )
    picked = jnp.dot(place, grads, preferred_element_type=jnp.float32)
    packed = (gate * picked).astype(jnp.bfloat16)
    outgoing = (
        packed.reshape(experts, slots_per, split, quarter)
        .transpose(0, 2, 1, 3)
        .reshape(count * slots_per, quarter)
    )

    outgoing, upper, target = lax.optimization_barrier((outgoing, grads[:half], target))
    upper_after = to_previous(upper)
    target_after = to_previous(target)
    rows = exchange(outgoing, "expert")
    rows, upper_after, target_after = lax.optimization_barrier((rows, upper_after, target_after))

    partial_value = lax.dot_general(
        rows, w_down[0], (((1,), (1,)), ((), ())), preferred_element_type=jnp.float32
    ).astype(jnp.bfloat16)
    pre = saved_pre[0, 0, 0]
    act = gelu_parts(pre)[0].astype(jnp.bfloat16)
    term_down = lax.dot_general(
        act, rows, (((0,), (0,)), ((), ())), preferred_element_type=jnp.float32
    ).astype(jnp.bfloat16)
    down_scattered = scatter_over_groups(term_down)

    part = lax.axis_index("expert") % split
    _, slope = gelu_parts(lax.dynamic_slice_in_dim(pre, part * share, share, 0))
    partial_value, lower = lax.optimization_barrier((partial_value, grads[half:]))
    lower_after = to_previous(lower)
    shares = exchange(partial_value, "expert", members)
    shares, lower_after = lax.optimization_barrier((shares, lower_after))
    own_grad = (
        jnp.sum(shares.reshape(split, share, -1).astype(jnp.float32), axis=0) * slope
    ).astype(jnp.bfloat16)
    hidden_grad = lax.all_gather(own_grad, "expert", axis_index_groups=members, tiled=True)

    back = lax.dot_general(
        hidden_grad, w_up[0], (((1,), (1,)), ((), ())), preferred_element_type=jnp.float32
    ).astype(jnp.bfloat16)
    returned = exchange(back, "expert")
    term_up = lax.dot_general(
        hidden_grad, saved_in[0, 0], (((0,), (0,)), ((), ())), preferred_element_type=jnp.float32
    ).astype(jnp.bfloat16)
    returned, term_up = lax.optimization_barrier((returned, term_up))
    returned = to_previous(returned)
    up = sum_over_groups(term_up)
    down = finish_groups(down_scattered)

    unpacked = (
        returned.reshape(experts, split, slots_per, quarter)
        .transpose(0, 2, 1, 3)
        .reshape(all_slots, width)
    )
    hit_after = [target_after[:, k][:, None] == slot_ids[None, :] for k in range(2)]
    place_after = (hit_after[0] | hit_after[1]).astype(jnp.bfloat16)
    grads_after = jnp.concatenate([upper_after, lower_after], axis=0)
    total = grads_after.astype(jnp.float32) + jnp.dot(
        place_after, unpacked, preferred_element_type=jnp.float32
    )
    return (total.astype(jnp.bfloat16)[None], up[None], down[None])


def solution(mesh):
    in_specs = (
        P("phase", ("dp", "expert"), None),
        P("phase", ("dp", "expert"), None),
        P("phase", ("dp", "expert"), None),
        P("phase", "dp", None, "expert"),
        P("phase", "dp", "expert", None, None),
        P("phase", "expert", None),
        P("phase", None, "expert"),
    )
    out_specs = (
        P("phase", ("dp", "expert"), None),
        P("phase", "dp", "expert"),
        P("phase", "dp", "expert"),
    )
    return jax.shard_map(body, mesh=mesh, in_specs=in_specs, out_specs=out_specs, check_vma=False)
```

```python
import jax
import jax.numpy as jnp
from jax import lax
from jax.sharding import PartitionSpec as P


def gelu_parts(pre):
    value = pre.astype(jnp.float32)
    cdf = 0.5 * (1.0 + lax.erf(value * 0.7071067811865476))
    dens = jnp.exp(-0.5 * value * value) * 0.3989422804014327
    return (value * cdf, cdf + value * dens)


def exchange(x, axis, groups=None):
    return lax.all_to_all(x, axis, 0, 0, tiled=True, axis_index_groups=groups)


def to_previous(x):
    peers = lax.axis_size("phase")
    return lax.ppermute(x, "phase", [(i, i - 1) for i in range(1, peers)])


def slot_targets(chosen, experts, slots_per):
    tokens = chosen.shape[0]
    flat = chosen.reshape(-1)
    onehot = (flat[:, None] == jnp.arange(experts, dtype=jnp.int32)[None, :]).astype(jnp.int32)
    before = jnp.cumsum(onehot, axis=0) - onehot
    slot = jnp.sum(before * onehot, axis=1)
    return (flat * slots_per + slot).reshape(tokens, 2)


def along_z(term, steps):
    count = lax.axis_size("dp")
    near = count // 2
    hid, quarter = term.shape
    blocks = term.reshape(2, near, hid // count, quarter)
    here = lax.axis_index("dp") % near
    arrived = []
    for k in steps:
        block = lax.dynamic_index_in_dim(blocks, (here + k) % near, 1, keepdims=False)
        block = block.reshape(hid // near, quarter)
        if k:
            pairs = [
                (h * near + z, h * near + (z + k) % near) for h in range(2) for z in range(near)
            ]
            block = lax.ppermute(block, "dp", pairs)
        arrived.append(block)
    return arrived


def add_up(blocks):
    total = blocks[0].astype(jnp.float32)
    for block in blocks[1:]:
        total = total + block.astype(jnp.float32)
    return total


def across_x(sums):
    count = lax.axis_size("dp")
    near = count // 2
    side = lax.axis_index("dp") // near
    both = jnp.stack([s.reshape(2, s.shape[0] // 2, s.shape[1]) for s in sums], axis=1)
    away = jnp.where(side == 1, both[0], both[1]).astype(jnp.bfloat16)
    keep = jnp.where(side == 1, both[1], both[0])
    got = lax.ppermute(away, "dp", [(i, (i + near) % count) for i in range(count)])
    out = (keep + got.astype(jnp.float32)).astype(jnp.bfloat16)
    return [out[i] for i in range(len(sums))]


def hold(*values):
    return lax.optimization_barrier(values)


def body(grad_out, routes, gates, saved_in, saved_pre, w_up, w_down):
    count = lax.axis_size("expert")
    grads = grad_out[0]
    chosen = routes[0]
    weights = gates[0]
    tokens, width = grads.shape
    quarter = w_up.shape[1]
    split = width // quarter
    experts = count // split
    slots_per = saved_in.shape[2] // count
    all_slots = experts * slots_per
    members = [[e * split + q for q in range(split)] for e in range(experts)]
    share = count * slots_per // split
    near = lax.axis_size("dp") // 2
    steps = sorted(range(1, near), key=lambda k: min(k, near - k))
    short, long = steps[: near // 2], steps[near // 2 :]
    cuts = (tokens // 2, tokens * 3 // 4)

    target = slot_targets(chosen, experts, slots_per)
    slot_ids = jnp.arange(all_slots, dtype=jnp.int32)
    hit = [(target[:, k][None, :] == slot_ids[:, None]) for k in range(2)]
    place = (hit[0] | hit[1]).astype(jnp.bfloat16)
    gate = jnp.sum(
        jnp.where(hit[0], weights[:, 0][None, :], 0.0)
        + jnp.where(hit[1], weights[:, 1][None, :], 0.0),
        axis=1,
        keepdims=True,
    )
    picked = jnp.dot(place, grads, preferred_element_type=jnp.float32)
    packed = (gate * picked).astype(jnp.bfloat16)
    outgoing = (
        packed.reshape(experts, slots_per, split, quarter)
        .transpose(0, 2, 1, 3)
        .reshape(count * slots_per, quarter)
    )

    outgoing, target, first_part = hold(outgoing, target, grads[: cuts[0]])
    first_after = to_previous(first_part)
    target_after = to_previous(target)
    rows = exchange(outgoing, "expert")
    rows, first_after, target_after = hold(rows, first_after, target_after)

    partial_value = lax.dot_general(
        rows, w_down[0], (((1,), (1,)), ((), ())), preferred_element_type=jnp.float32
    ).astype(jnp.bfloat16)
    pre = saved_pre[0, 0, 0]
    act = gelu_parts(pre)[0].astype(jnp.bfloat16)
    term_down = lax.dot_general(
        act, rows, (((0,), (0,)), ((), ())), preferred_element_type=jnp.float32
    ).astype(jnp.bfloat16)
    part = lax.axis_index("expert") % split
    _, slope = gelu_parts(lax.dynamic_slice_in_dim(pre, part * share, share, 0))
    partial_value, second_part = hold(partial_value, grads[cuts[0] : cuts[1]])
    shares = exchange(partial_value, "expert", members)
    second_after = to_previous(second_part)
    down_blocks = along_z(term_down, [0] + short)
    shares, second_after, *down_blocks = hold(shares, second_after, *down_blocks)
    own_grad = (
        jnp.sum(shares.reshape(split, share, -1).astype(jnp.float32), axis=0) * slope
    ).astype(jnp.bfloat16)
    own_grad, third_part, term_down = hold(own_grad, grads[cuts[1] :], term_down)
    hidden_grad = exchange(jnp.tile(own_grad, (split, 1)), "expert", members)
    third_after = to_previous(third_part)
    down_rest = along_z(term_down, long)
    hidden_grad, third_after, *down_rest = hold(hidden_grad, third_after, *down_rest)

    back = lax.dot_general(
        hidden_grad, w_up[0], (((1,), (1,)), ((), ())), preferred_element_type=jnp.float32
    ).astype(jnp.bfloat16)
    term_up = lax.dot_general(
        hidden_grad, saved_in[0, 0], (((0,), (0,)), ((), ())), preferred_element_type=jnp.float32
    ).astype(jnp.bfloat16)
    returned = exchange(back, "expert")
    up_blocks = along_z(term_up, [0] + short)
    returned, term_up, *up_blocks = hold(returned, term_up, *up_blocks)
    returned = to_previous(returned)
    up_rest = along_z(term_up, long)
    returned, *up_rest = hold(returned, *up_rest)
    down, up = across_x([add_up(down_blocks + down_rest), add_up(up_blocks + up_rest)])

    unpacked = (
        returned.reshape(experts, split, slots_per, quarter)
        .transpose(0, 2, 1, 3)
        .reshape(all_slots, width)
    )
    hit_after = [target_after[:, k][:, None] == slot_ids[None, :] for k in range(2)]
    place_after = (hit_after[0] | hit_after[1]).astype(jnp.bfloat16)
    grads_after = jnp.concatenate([first_after, second_after, third_after], axis=0)
    total = grads_after.astype(jnp.float32) + jnp.dot(
        place_after, unpacked, preferred_element_type=jnp.float32
    )
    return (total.astype(jnp.bfloat16)[None], up[None], down[None])


def solution(mesh):
    in_specs = (
        P("phase", ("dp", "expert"), None),
        P("phase", ("dp", "expert"), None),
        P("phase", ("dp", "expert"), None),
        P("phase", "dp", None, "expert"),
        P("phase", "dp", "expert", None, None),
        P("phase", "expert", None),
        P("phase", None, "expert"),
    )
    out_specs = (
        P("phase", ("dp", "expert"), None),
        P("phase", "dp", "expert"),
        P("phase", "dp", "expert"),
    )
    return jax.shard_map(body, mesh=mesh, in_specs=in_specs, out_specs=out_specs, check_vma=False)
```

```python
import jax
import jax.numpy as jnp
from jax import lax
from jax.sharding import PartitionSpec as P


def gelu_parts(pre):
    value = pre.astype(jnp.float32)
    cdf = 0.5 * (1.0 + lax.erf(value * 0.7071067811865476))
    dens = jnp.exp(-0.5 * value * value) * 0.3989422804014327
    return (value * cdf, cdf + value * dens)


def exchange(x, axis, groups=None):
    return lax.all_to_all(x, axis, 0, 0, tiled=True, axis_index_groups=groups)


def to_previous(x):
    peers = lax.axis_size("phase")
    return lax.ppermute(x, "phase", [(i, i - 1) for i in range(1, peers)])


def partner(block, axis, bit):
    count = lax.axis_size(axis)
    return lax.ppermute(block, axis, [(i, i ^ (1 << bit)) for i in range(count)])


def hold(*values):
    return lax.optimization_barrier(values)


def slot_targets(chosen, experts, slots_per):
    tokens = chosen.shape[0]
    flat = chosen.reshape(-1)
    onehot = (flat[:, None] == jnp.arange(experts, dtype=jnp.int32)[None, :]).astype(jnp.int32)
    before = jnp.cumsum(onehot, axis=0) - onehot
    slot = jnp.sum(before * onehot, axis=1)
    return (flat * slots_per + slot).reshape(tokens, 2)


def exchange_pieces(term):
    return exchange(term, "dp")


def add_pieces(pieces):
    count = lax.axis_size("dp")
    hid, quarter = pieces.shape
    pieces = pieces.reshape(count, hid // count, quarter)
    return jnp.sum(pieces.astype(jnp.float32), axis=0).astype(jnp.bfloat16)


def split_by(mine, lower, upper):
    keep = jnp.where(mine == 1, upper, lower)
    away = jnp.where(mine == 1, lower, upper)
    return keep, away


def gather_columns(buffer, levels, position):
    size = buffer.shape[0]
    rest = buffer.shape[1:]
    for level in range(levels):
        mine = position >> level & 1
        shaped = buffer.reshape((size >> level + 1, 2, 1 << level) + rest)
        keep, away = split_by(mine, shaped[:, 0], shaped[:, 1])
        got = partner(away, "expert", level)
        first = jnp.where(mine == 1, got, keep)
        second = jnp.where(mine == 1, keep, got)
        buffer = jnp.stack([first, second], axis=1).reshape((size,) + rest)
    return buffer


def behind(block, flip):
    sections = lax.axis_size("phase")
    count = lax.axis_size("expert")
    pairs = [
        (s * count + i, (s - 1) * count + (i ^ flip)) for s in range(1, sections) for i in range(count)
    ]
    return lax.ppermute(block, ("phase", "expert"), pairs)


def body(grad_out, routes, gates, saved_in, saved_pre, w_up, w_down):
    count = lax.axis_size("expert")
    position = lax.axis_index("expert")
    grads = grad_out[0]
    chosen = routes[0]
    weights = gates[0]
    tokens, width = grads.shape
    quarter = w_up.shape[1]
    split = width // quarter
    experts = count // split
    slots_per = saved_in.shape[2] // count
    all_slots = experts * slots_per
    levels = split.bit_length() - 1
    cut = tokens // 2
    rows_all = count * slots_per

    target = slot_targets(chosen, experts, slots_per)
    slot_ids = jnp.arange(all_slots, dtype=jnp.int32)
    hit = [(target[:, k][None, :] == slot_ids[:, None]) for k in range(2)]
    place = (hit[0] | hit[1]).astype(jnp.bfloat16)
    gate = jnp.sum(
        jnp.where(hit[0], weights[:, 0][None, :], 0.0)
        + jnp.where(hit[1], weights[:, 1][None, :], 0.0),
        axis=1,
        keepdims=True,
    )
    picked = jnp.dot(place, grads, preferred_element_type=jnp.float32)
    packed = (gate * picked).astype(jnp.bfloat16)
    outgoing = (
        packed.reshape(experts, slots_per, split, quarter)
        .transpose(0, 2, 1, 3)
        .reshape(count * slots_per, quarter)
    )
    mark = jnp.pad(place, ((0, 0), (0, width - tokens)))

    first_part = jnp.concatenate([mark, grads[:cut]], axis=0)
    outgoing, first_part = hold(outgoing, first_part)
    first_after = to_previous(first_part)
    rows = exchange(outgoing, "expert")
    rows, first_after = hold(rows, first_after)

    partial_value = lax.dot_general(
        rows, w_down[0], (((1,), (1,)), ((), ())), preferred_element_type=jnp.float32
    )
    pre = saved_pre[0, 0, 0]
    act, slope = gelu_parts(pre)
    act = act.astype(jnp.bfloat16)
    term_down = lax.dot_general(
        act, rows, (((0,), (0,)), ((), ())), preferred_element_type=jnp.float32
    ).astype(jnp.bfloat16)
    down_pieces = exchange_pieces(term_down)

    core = position & 1
    half = rows_all // 2
    keep, away = split_by(core, partial_value[:half], partial_value[half:])
    value = keep + partner(away.astype(jnp.bfloat16), "expert", 0).astype(jnp.float32)
    for level in range(1, levels):
        value = value + partner(value.astype(jnp.bfloat16), "expert", level).astype(jnp.float32)
    own_slope = jnp.where(core == 1, slope[half:], slope[:half])
    own_grad = (value * own_slope).astype(jnp.bfloat16)
    other_grad = partner(own_grad, "expert", 0)
    hidden_grad = jnp.concatenate(
        [jnp.where(core == 1, other_grad, own_grad), jnp.where(core == 1, own_grad, other_grad)],
        axis=0,
    )
    second_after = to_previous(grads[cut:])
    hidden_grad, second_after = hold(hidden_grad, second_after)

    term_up = lax.dot_general(
        hidden_grad, saved_in[0, 0], (((0,), (0,)), ((), ())), preferred_element_type=jnp.float32
    ).astype(jnp.bfloat16)
    back = lax.dot_general(
        hidden_grad, w_up[0], (((1,), (1,)), ((), ())), preferred_element_type=jnp.float32
    ).astype(jnp.bfloat16)
    term_up, down_pieces = hold(term_up, down_pieces)
    up_pieces = exchange_pieces(term_up)
    down = add_pieces(down_pieces)

    shaped = back.reshape(experts, split, slots_per, quarter).transpose(1, 0, 2, 3)
    gathered = gather_columns(shaped, levels, position)
    mine = position >> levels
    keep, away = split_by(mine, gathered[:, 0], gathered[:, 1])
    kept = behind(keep, 0)
    got = behind(away, split)
    first = jnp.where(mine == 1, got, kept)
    second = jnp.where(mine == 1, kept, got)
    unpacked = (
        jnp.stack([first, second], axis=0).transpose(0, 2, 1, 3).reshape(all_slots, width)
    )
    place_after = first_after[:all_slots, :tokens]
    grads_after = jnp.concatenate([first_after[all_slots:], second_after], axis=0)
    total = grads_after.astype(jnp.float32) + lax.dot_general(
        place_after, unpacked, (((0,), (0,)), ((), ())), preferred_element_type=jnp.float32
    )
    up = add_pieces(up_pieces)
    return (total.astype(jnp.bfloat16)[None], up[None], down[None])


def solution(mesh):
    in_specs = (
        P("phase", ("dp", "expert"), None),
        P("phase", ("dp", "expert"), None),
        P("phase", ("dp", "expert"), None),
        P("phase", "dp", None, "expert"),
        P("phase", "dp", "expert", None, None),
        P("phase", "expert", None),
        P("phase", None, "expert"),
    )
    out_specs = (
        P("phase", ("dp", "expert"), None),
        P("phase", "dp", "expert"),
        P("phase", "dp", "expert"),
    )
    return jax.shard_map(body, mesh=mesh, in_specs=in_specs, out_specs=out_specs, check_vma=False)
```

```python
import jax
import jax.numpy as jnp
from jax import lax
from jax.sharding import PartitionSpec as P


def gelu_parts(pre):
    value = pre.astype(jnp.float32)
    cdf = 0.5 * (1.0 + lax.erf(value * 0.7071067811865476))
    dens = jnp.exp(-0.5 * value * value) * 0.3989422804014327
    return (value * cdf, cdf + value * dens)


def exchange(x, axis, groups=None):
    return lax.all_to_all(x, axis, 0, 0, tiled=True, axis_index_groups=groups)


def to_previous(x):
    peers = lax.axis_size("phase")
    return lax.ppermute(x, "phase", [(i, i - 1) for i in range(1, peers)])


def partner(block, axis, bit):
    count = lax.axis_size(axis)
    return lax.ppermute(block, axis, [(i, i ^ (1 << bit)) for i in range(count)])


def hold(*values):
    return lax.optimization_barrier(values)


def slot_targets(chosen, experts, slots_per):
    tokens = chosen.shape[0]
    flat = chosen.reshape(-1)
    onehot = (flat[:, None] == jnp.arange(experts, dtype=jnp.int32)[None, :]).astype(jnp.int32)
    before = jnp.cumsum(onehot, axis=0) - onehot
    slot = jnp.sum(before * onehot, axis=1)
    return (flat * slots_per + slot).reshape(tokens, 2)


def scatter_along_z(term):
    count = lax.axis_size("dp")
    near = count // 2
    hid, quarter = term.shape
    groups = [[h * near + z for z in range(near)] for h in range(2)]
    ordered = term.reshape(2, near, hid // count, quarter).transpose(1, 0, 2, 3)
    return exchange(ordered.reshape(hid, quarter), "dp", groups)


def add_pieces(pieces):
    near = lax.axis_size("dp") // 2
    hid, quarter = pieces.shape
    pieces = pieces.reshape(near, 2, hid // (2 * near), quarter)
    return jnp.sum(pieces.astype(jnp.float32), axis=0)


def across_x(sums):
    count = lax.axis_size("dp")
    near = count // 2
    side = lax.axis_index("dp") // near
    away = jnp.stack([jnp.where(side == 1, s[0], s[1]).astype(jnp.bfloat16) for s in sums])
    got = lax.ppermute(away, "dp", [(i, (i + near) % count) for i in range(count)])
    return [
        (jnp.where(side == 1, s[1], s[0]) + got[i].astype(jnp.float32)).astype(jnp.bfloat16)
        for i, s in enumerate(sums)
    ]


def split_by(mine, lower, upper):
    keep = jnp.where(mine == 1, upper, lower)
    away = jnp.where(mine == 1, lower, upper)
    return keep, away


def behind(block, flip):
    sections = lax.axis_size("phase")
    count = lax.axis_size("expert")
    pairs = [
        (s * count + i, (s - 1) * count + (i ^ flip)) for s in range(1, sections) for i in range(count)
    ]
    return lax.ppermute(block, ("phase", "expert"), pairs)


def body(grad_out, routes, gates, saved_in, saved_pre, w_up, w_down):
    count = lax.axis_size("expert")
    position = lax.axis_index("expert")
    grads = grad_out[0]
    chosen = routes[0]
    weights = gates[0]
    tokens, width = grads.shape
    quarter = w_up.shape[1]
    split = width // quarter
    experts = count // split
    slots_per = saved_in.shape[2] // count
    all_slots = experts * slots_per
    levels = split.bit_length() - 1
    rows_all = count * slots_per

    target = slot_targets(chosen, experts, slots_per)
    slot_ids = jnp.arange(all_slots, dtype=jnp.int32)
    hit = [(target[:, k][None, :] == slot_ids[:, None]) for k in range(2)]
    place = (hit[0] | hit[1]).astype(jnp.bfloat16)
    gate = jnp.sum(
        jnp.where(hit[0], weights[:, 0][None, :], 0.0)
        + jnp.where(hit[1], weights[:, 1][None, :], 0.0),
        axis=1,
        keepdims=True,
    )
    picked = jnp.dot(place, grads, preferred_element_type=jnp.float32)
    packed = (gate * picked).astype(jnp.bfloat16)
    outgoing = (
        packed.reshape(experts, slots_per, split, quarter)
        .transpose(0, 2, 1, 3)
        .reshape(count * slots_per, quarter)
    )
    outgoing, place = hold(outgoing, place)
    place_after = to_previous(place)
    rows = exchange(outgoing, "expert")
    rows, place_after = hold(rows, place_after)

    partial_value = lax.dot_general(
        rows, w_down[0], (((1,), (1,)), ((), ())), preferred_element_type=jnp.float32
    )
    pre = saved_pre[0, 0, 0]
    act, slope = gelu_parts(pre)
    act = act.astype(jnp.bfloat16)
    term_down = lax.dot_general(
        act, rows, (((0,), (0,)), ((), ())), preferred_element_type=jnp.float32
    ).astype(jnp.bfloat16)
    down_pieces = scatter_along_z(term_down)

    core = position & 1
    half = rows_all // 2
    keep, away = split_by(core, partial_value[:half], partial_value[half:])
    value = keep + partner(away.astype(jnp.bfloat16), "expert", 0).astype(jnp.float32)
    for level in range(1, levels):
        value = value + partner(value.astype(jnp.bfloat16), "expert", level).astype(jnp.float32)
    own_slope = jnp.where(core == 1, slope[half:], slope[:half])
    own_grad = (value * own_slope).astype(jnp.bfloat16)
    other_grad = partner(own_grad, "expert", 0)
    hidden_grad = jnp.concatenate(
        [jnp.where(core == 1, other_grad, own_grad), jnp.where(core == 1, own_grad, other_grad)],
        axis=0,
    )
    hidden_grad, down_pieces = hold(hidden_grad, down_pieces)
    grads_after = to_previous(grads)

    term_up = lax.dot_general(
        hidden_grad, saved_in[0, 0], (((0,), (0,)), ((), ())), preferred_element_type=jnp.float32
    ).astype(jnp.bfloat16)
    out_block = jnp.arange(rows_all, dtype=jnp.int32)[:, None]
    in_block = jnp.arange(rows_all, dtype=jnp.int32)[None, :]
    bits = levels + 1
    goes = sum(
        (out_block // slots_per >> (bits - 1 - b) & 1) << b for b in range(bits)
    )
    same = ((goes ^ position) == in_block // slots_per) & (
        out_block % slots_per == in_block % slots_per
    )
    ordered = jnp.dot(
        same.astype(jnp.bfloat16), hidden_grad, preferred_element_type=jnp.float32
    ).astype(jnp.bfloat16)
    back = lax.dot_general(
        ordered, w_up[0], (((1,), (1,)), ((), ())), preferred_element_type=jnp.float32
    ).astype(jnp.bfloat16)
    up_pieces = scatter_along_z(term_up)

    buffer = back.reshape(1, count, slots_per, quarter)
    for level in range(levels):
        middle = buffer.shape[1] // 2
        got = partner(buffer[:, middle:], "expert", level)
        buffer = jnp.concatenate([buffer[:, :middle], got], axis=0)
        if level == 0:
            buffer, grads_after = hold(buffer, grads_after)
    kept = behind(buffer[:, 0], 0)
    got = behind(buffer[:, 1], split)
    blocks = jnp.stack([kept, got]).transpose(0, 2, 1, 3)
    for level in range(levels):
        shaped = blocks.reshape(
            experts, slots_per, split >> (level + 1), 2, 1 << level, quarter
        )
        blocks = jnp.where((position >> level & 1) == 1, jnp.flip(shaped, 3), shaped)
    unpacked = blocks.reshape(all_slots, width)
    mine = position >> levels
    place_after = place_after.reshape(experts, slots_per, tokens)
    place_after = jnp.where(mine == 1, place_after[::-1], place_after).reshape(all_slots, tokens)
    total = grads_after.astype(jnp.float32) + lax.dot_general(
        place_after, unpacked, (((0,), (0,)), ((), ())), preferred_element_type=jnp.float32
    )
    down, up = across_x([add_pieces(down_pieces), add_pieces(up_pieces)])
    return (total.astype(jnp.bfloat16)[None], up[None], down[None])


def solution(mesh):
    in_specs = (
        P("phase", ("dp", "expert"), None),
        P("phase", ("dp", "expert"), None),
        P("phase", ("dp", "expert"), None),
        P("phase", "dp", None, "expert"),
        P("phase", "dp", "expert", None, None),
        P("phase", "expert", None),
        P("phase", None, "expert"),
    )
    out_specs = (
        P("phase", ("dp", "expert"), None),
        P("phase", "dp", "expert"),
        P("phase", "dp", "expert"),
    )
    return jax.shard_map(body, mesh=mesh, in_specs=in_specs, out_specs=out_specs, check_vma=False)
```

```python
import jax
import jax.numpy as jnp
from jax import lax
from jax.experimental import pallas as pl
from jax.experimental.pallas import tpu as pltpu
from jax.sharding import PartitionSpec as P


def gelu_parts(pre):
    value = pre.astype(jnp.float32)
    cdf = 0.5 * (1.0 + lax.erf(value * 0.7071067811865476))
    dens = jnp.exp(-0.5 * value * value) * 0.3989422804014327
    return (value * cdf, cdf + value * dens)


def exchange(x, axis, groups=None):
    return lax.all_to_all(x, axis, 0, 0, tiled=True, axis_index_groups=groups)


def to_previous(x):
    peers = lax.axis_size("phase")
    return lax.ppermute(x, "phase", [(i, i - 1) for i in range(1, peers)])


def partner(block, axis, bit):
    count = lax.axis_size(axis)
    return lax.ppermute(block, axis, [(i, i ^ (1 << bit)) for i in range(count)])


def hold(*values):
    return lax.optimization_barrier(values)


def scatter_along_z(term):
    count = lax.axis_size("dp")
    near = count // 2
    hid, quarter = term.shape
    groups = [[h * near + z for z in range(near)] for h in range(2)]
    ordered = term.reshape(2, near, hid // count, quarter).transpose(1, 0, 2, 3)
    return exchange(ordered.reshape(hid, quarter), "dp", groups)


def add_pieces(pieces):
    near = lax.axis_size("dp") // 2
    hid, quarter = pieces.shape
    pieces = pieces.reshape(near, 2, hid // (2 * near), quarter)
    return jnp.sum(pieces.astype(jnp.float32), axis=0)


def leaving_x(sums):
    side = lax.axis_index("dp") // (lax.axis_size("dp") // 2)
    return jnp.stack([jnp.where(side == 1, s[0], s[1]).astype(jnp.bfloat16) for s in sums])


def across_x(sums, away):
    count = lax.axis_size("dp")
    near = count // 2
    side = lax.axis_index("dp") // near
    got = lax.ppermute(away, "dp", [(i, (i + near) % count) for i in range(count)])
    return [
        (jnp.where(side == 1, s[1], s[0]) + got[i].astype(jnp.float32)).astype(jnp.bfloat16)
        for i, s in enumerate(sums)
    ]


def split_by(mine, lower, upper):
    keep = jnp.where(mine == 1, upper, lower)
    away = jnp.where(mine == 1, lower, upper)
    return keep, away


def behind(block, flip):
    sections = lax.axis_size("phase")
    count = lax.axis_size("expert")
    pairs = [
        (s * count + i, (s - 1) * count + (i ^ flip)) for s in range(1, sections) for i in range(count)
    ]
    return lax.ppermute(block, ("phase", "expert"), pairs)


def combine_kernel(spot, grads, place, kept, got, out):
    quarter = kept.shape[2]
    odd = spot[0] & 1
    for c in range(2):
        columns = slice(c * quarter, (c + 1) * quarter)
        rows = jnp.concatenate([kept[c ^ odd], got[c ^ odd]], axis=0)
        added = jnp.dot(place[...], rows, preferred_element_type=jnp.float32)
        out[:, columns] = (grads[:, columns].astype(jnp.float32) + added).astype(out.dtype)


def combine(spot, grads, place, kept, got):
    tokens, width = grads.shape
    split, slots_per, quarter = kept.shape
    wide = pl.BlockSpec((tokens, 2 * quarter), lambda i, spot: (0, i ^ (spot[0] >> 1)))
    pair = pl.BlockSpec((2, slots_per, quarter), lambda i, spot: (i, 0, 0))
    return pl.pallas_call(
        combine_kernel,
        grid_spec=pltpu.PrefetchScalarGridSpec(
            num_scalar_prefetch=1,
            grid=(split // 2,),
            in_specs=[wide, pl.BlockSpec(place.shape, lambda i, spot: (0, 0)), pair, pair],
            out_specs=wide,
        ),
        out_shape=jax.ShapeDtypeStruct(grads.shape, grads.dtype),
        cost_estimate=pl.CostEstimate(
            flops=4 * tokens * slots_per * width,
            bytes_accessed=4 * tokens * width + 4 * slots_per * width,
            transcendentals=0,
        ),
        name="combine",
    )(spot.astype(jnp.int32).reshape(1), grads, place, kept, got)


def body(grad_out, routes, gates, saved_in, saved_pre, w_up, w_down):
    count = lax.axis_size("expert")
    position = lax.axis_index("expert")
    grads = grad_out[0]
    chosen = routes[0]
    weights = gates[0]
    tokens, width = grads.shape
    quarter = w_up.shape[1]
    split = width // quarter
    experts = count // split
    slots_per = saved_in.shape[2] // count
    all_slots = experts * slots_per
    levels = split.bit_length() - 1
    rows_all = count * slots_per

    expert_ids = jnp.arange(experts, dtype=jnp.int32)[:, None]
    slot_ids = jnp.arange(slots_per, dtype=jnp.int32)[None, :, None]
    names = [chosen[:, k][None, :] == expert_ids for k in range(2)]
    named = names[0] | names[1]
    token_ids = jnp.arange(tokens, dtype=jnp.int32)
    earlier = (token_ids[:, None] < token_ids[None, :]).astype(jnp.bfloat16)
    slot = jnp.dot(
        named.astype(jnp.bfloat16), earlier, preferred_element_type=jnp.float32
    ).astype(jnp.int32)
    hit = named[:, None, :] & (slot[:, None, :] == slot_ids)
    place = hit.astype(jnp.bfloat16).reshape(all_slots, tokens)
    pair_gate = jnp.where(names[0], weights[:, 0][None, :], weights[:, 1][None, :])
    gate = jnp.sum(jnp.where(hit, pair_gate[:, None, :], 0.0), axis=2).reshape(all_slots, 1)
    picked = jnp.dot(place, grads, preferred_element_type=jnp.float32)
    packed = (gate * picked).astype(jnp.bfloat16)
    outgoing = (
        packed.reshape(experts, slots_per, split, quarter)
        .transpose(0, 2, 1, 3)
        .reshape(count * slots_per, quarter)
    )
    outgoing, place = hold(outgoing, place)
    place_after = to_previous(place)
    rows = exchange(outgoing, "expert")
    rows, place_after = hold(rows, place_after)

    partial_value = lax.dot_general(
        rows, w_down[0], (((1,), (1,)), ((), ())), preferred_element_type=jnp.float32
    )
    pre = saved_pre[0, 0, 0]
    act, slope = gelu_parts(pre)
    act = act.astype(jnp.bfloat16)
    term_down = lax.dot_general(
        act, rows, (((0,), (0,)), ((), ())), preferred_element_type=jnp.float32
    ).astype(jnp.bfloat16)

    core = position & 1
    half = rows_all // 2
    keep, away = split_by(core, partial_value[:half], partial_value[half:])
    value = keep + partner(away.astype(jnp.bfloat16), "expert", 0).astype(jnp.float32)
    value, term_down = hold(value, term_down)
    down_pieces = scatter_along_z(term_down)
    for level in range(1, levels):
        value = value + partner(value.astype(jnp.bfloat16), "expert", level).astype(jnp.float32)
    own_slope = jnp.where(core == 1, slope[half:], slope[:half])
    own_grad = (value * own_slope).astype(jnp.bfloat16)
    other_grad = partner(own_grad, "expert", 0)
    hidden_grad = jnp.concatenate(
        [jnp.where(core == 1, other_grad, own_grad), jnp.where(core == 1, own_grad, other_grad)],
        axis=0,
    )
    grads_after = to_previous(grads)

    term_up = lax.dot_general(
        hidden_grad, saved_in[0, 0], (((0,), (0,)), ((), ())), preferred_element_type=jnp.float32
    ).astype(jnp.bfloat16)
    out_block = jnp.arange(rows_all, dtype=jnp.int32)[:, None]
    in_block = jnp.arange(rows_all, dtype=jnp.int32)[None, :]
    bits = levels + 1
    goes = sum(
        (out_block // slots_per >> (bits - 1 - b) & 1) << b for b in range(bits)
    )
    same = ((goes ^ position) == in_block // slots_per) & (
        out_block % slots_per == in_block % slots_per
    )
    ordered = jnp.dot(
        same.astype(jnp.bfloat16), hidden_grad, preferred_element_type=jnp.float32
    ).astype(jnp.bfloat16)
    back = lax.dot_general(
        ordered, w_up[0], (((1,), (1,)), ((), ())), preferred_element_type=jnp.float32
    ).astype(jnp.bfloat16)

    buffer = back.reshape(1, count, slots_per, quarter)
    for level in range(levels):
        middle = buffer.shape[1] // 2
        got = partner(buffer[:, middle:], "expert", level)
        buffer = jnp.concatenate([buffer[:, :middle], got], axis=0)
        if level == 0:
            buffer, down_pieces, term_up = hold(buffer, down_pieces, term_up)
            up_pieces = scatter_along_z(term_up)
        if level == 1:
            buffer, grads_after = hold(buffer, grads_after)
    kept = behind(buffer[:, 0], 0)
    got = behind(buffer[:, 1], split)
    sums = [add_pieces(down_pieces), add_pieces(up_pieces)]
    kept, got, away = hold(kept, got, leaving_x(sums))
    mine = position >> levels
    place_after = place_after.reshape(experts, slots_per, tokens)
    place_after = jnp.where(mine == 1, place_after[::-1], place_after).reshape(all_slots, tokens)
    total = combine(position & (split - 1), grads_after, place_after.T, kept, got)
    down, up = across_x(sums, away)
    return (total[None], up[None], down[None])


def solution(mesh):
    in_specs = (
        P("phase", ("dp", "expert"), None),
        P("phase", ("dp", "expert"), None),
        P("phase", ("dp", "expert"), None),
        P("phase", "dp", None, "expert"),
        P("phase", "dp", "expert", None, None),
        P("phase", "expert", None),
        P("phase", None, "expert"),
    )
    out_specs = (
        P("phase", ("dp", "expert"), None),
        P("phase", "dp", "expert"),
        P("phase", "dp", "expert"),
    )
    return jax.shard_map(body, mesh=mesh, in_specs=in_specs, out_specs=out_specs, check_vma=False)
```

```python
import jax
import jax.numpy as jnp
from jax import lax
from jax.experimental import pallas as pl
from jax.experimental.pallas import tpu as pltpu
from jax.sharding import PartitionSpec as P


def gelu_parts(pre):
    value = pre.astype(jnp.float32)
    cdf = 0.5 * (1.0 + lax.erf(value * 0.7071067811865476))
    dens = jnp.exp(-0.5 * value * value) * 0.3989422804014327
    return (value * cdf, cdf + value * dens)


def exchange(x, axis, groups=None):
    return lax.all_to_all(x, axis, 0, 0, tiled=True, axis_index_groups=groups)


def to_previous(x):
    peers = lax.axis_size("phase")
    return lax.ppermute(x, "phase", [(i, i - 1) for i in range(1, peers)])


def partner(block, axis, bit):
    count = lax.axis_size(axis)
    return lax.ppermute(block, axis, [(i, i ^ (1 << bit)) for i in range(count)])


def hold(*values):
    return lax.optimization_barrier(values)


def scatter_along_z(term):
    count = lax.axis_size("dp")
    near = count // 2
    hid, quarter = term.shape
    groups = [[h * near + z for z in range(near)] for h in range(2)]
    ordered = term.reshape(2, near, hid // count, quarter).transpose(1, 0, 2, 3)
    return exchange(ordered.reshape(hid, quarter), "dp", groups)


def add_pieces(pieces):
    near = lax.axis_size("dp") // 2
    hid, quarter = pieces.shape
    pieces = pieces.reshape(near, 2, hid // (2 * near), quarter)
    return jnp.sum(pieces.astype(jnp.float32), axis=0)


def leaving_x(sums):
    side = lax.axis_index("dp") // (lax.axis_size("dp") // 2)
    return jnp.stack([jnp.where(side == 1, s[0], s[1]).astype(jnp.bfloat16) for s in sums])


def across_x(away):
    count = lax.axis_size("dp")
    return lax.ppermute(away, "dp", [(i, (i + count // 2) % count) for i in range(count)])


def staying_x(sums, got):
    side = lax.axis_index("dp") // (lax.axis_size("dp") // 2)
    return [
        (jnp.where(side == 1, s[1], s[0]) + got[i].astype(jnp.float32)).astype(jnp.bfloat16)
        for i, s in enumerate(sums)
    ]


def split_by(mine, lower, upper):
    keep = jnp.where(mine == 1, upper, lower)
    away = jnp.where(mine == 1, lower, upper)
    return keep, away


def behind(block, flip):
    sections = lax.axis_size("phase")
    count = lax.axis_size("expert")
    pairs = [
        (s * count + i, (s - 1) * count + (i ^ flip)) for s in range(1, sections) for i in range(count)
    ]
    return lax.ppermute(block, ("phase", "expert"), pairs)


def combine_kernel(spot, grads, place, kept, got, out):
    quarter = kept.shape[2]
    odd = spot[0] & 1
    for c in range(2):
        columns = slice(c * quarter, (c + 1) * quarter)
        rows = jnp.concatenate([kept[c ^ odd], got[c ^ odd]], axis=0)
        added = jnp.dot(place[...], rows, preferred_element_type=jnp.float32)
        out[:, columns] = (grads[:, columns].astype(jnp.float32) + added).astype(out.dtype)


def combine(spot, grads, place, kept, got):
    tokens, width = grads.shape
    split, slots_per, quarter = kept.shape
    wide = pl.BlockSpec((tokens, 2 * quarter), lambda i, spot: (0, i ^ (spot[0] >> 1)))
    pair = pl.BlockSpec((2, slots_per, quarter), lambda i, spot: (i, 0, 0))
    return pl.pallas_call(
        combine_kernel,
        grid_spec=pltpu.PrefetchScalarGridSpec(
            num_scalar_prefetch=1,
            grid=(split // 2,),
            in_specs=[wide, pl.BlockSpec(place.shape, lambda i, spot: (0, 0)), pair, pair],
            out_specs=wide,
        ),
        out_shape=jax.ShapeDtypeStruct(grads.shape, grads.dtype),
        cost_estimate=pl.CostEstimate(
            flops=4 * tokens * slots_per * width,
            bytes_accessed=4 * tokens * width + 4 * slots_per * width,
            transcendentals=0,
        ),
        name="combine",
    )(spot.astype(jnp.int32).reshape(1), grads, place, kept, got)


def body(grad_out, routes, gates, saved_in, saved_pre, w_up, w_down):
    count = lax.axis_size("expert")
    position = lax.axis_index("expert")
    grads = grad_out[0]
    chosen = routes[0]
    weights = gates[0]
    tokens, width = grads.shape
    quarter = w_up.shape[1]
    split = width // quarter
    experts = count // split
    slots_per = saved_in.shape[2] // count
    all_slots = experts * slots_per
    levels = split.bit_length() - 1
    rows_all = count * slots_per

    expert_ids = jnp.arange(experts, dtype=jnp.int32)[:, None]
    slot_ids = jnp.arange(slots_per, dtype=jnp.int32)[None, :, None]
    names = chosen.T[:, None, :] == expert_ids[None]
    named = jnp.any(names, axis=0)
    token_ids = jnp.arange(tokens, dtype=jnp.int32)
    earlier = (token_ids[:, None] < token_ids[None, :]).astype(jnp.bfloat16)
    slot = jnp.dot(
        named.astype(jnp.bfloat16), earlier, preferred_element_type=jnp.float32
    ).astype(jnp.int32)
    hit = named[:, None, :] & (slot[:, None, :] == slot_ids)
    place = hit.astype(jnp.bfloat16).reshape(all_slots, tokens)
    pair_gate = jnp.sum(jnp.where(names, weights.T[:, None, :], 0.0), axis=0)
    gate = jnp.sum(jnp.where(hit, pair_gate[:, None, :], 0.0), axis=2).reshape(all_slots, 1)
    picked = jnp.dot(place, grads, preferred_element_type=jnp.float32)
    packed = (gate * picked).astype(jnp.bfloat16)
    outgoing = (
        packed.reshape(experts, slots_per, split, quarter)
        .transpose(0, 2, 1, 3)
        .reshape(count * slots_per, quarter)
    )
    swapped = place.reshape(experts, slots_per, tokens)[::-1].reshape(all_slots, tokens)
    place_after = to_previous(jnp.where(position >> levels == 1, swapped, place).T)
    rows = exchange(outgoing, "expert")
    rows, place_after = hold(rows, place_after)

    partial_value = lax.dot_general(
        rows, w_down[0], (((1,), (1,)), ((), ())), preferred_element_type=jnp.float32
    )
    pre = saved_pre[0, 0, 0]
    act, slope = gelu_parts(pre)
    act = act.astype(jnp.bfloat16)
    term_down = lax.dot_general(
        act, rows, (((0,), (0,)), ((), ())), preferred_element_type=jnp.float32
    ).astype(jnp.bfloat16)

    core = position & 1
    half = rows_all // 2
    keep, away = split_by(core, partial_value[:half], partial_value[half:])
    value = keep + partner(away.astype(jnp.bfloat16), "expert", 0).astype(jnp.float32)
    down_pieces = scatter_along_z(term_down)
    for level in range(1, levels):
        value = value + partner(value.astype(jnp.bfloat16), "expert", level).astype(jnp.float32)
    own_slope = jnp.where(core == 1, slope[half:], slope[:half])
    own_grad = (value * own_slope).astype(jnp.bfloat16)
    other_grad = partner(own_grad, "expert", 0)
    hidden_grad = jnp.concatenate(
        [jnp.where(core == 1, other_grad, own_grad), jnp.where(core == 1, own_grad, other_grad)],
        axis=0,
    )
    grads_after = to_previous(grads)

    hidden_grad, down_pieces = hold(hidden_grad, down_pieces)
    out_block = jnp.arange(rows_all, dtype=jnp.int32)[:, None]
    in_block = jnp.arange(rows_all, dtype=jnp.int32)[None, :]
    bits = levels + 1
    goes = sum(
        (out_block // slots_per >> (bits - 1 - b) & 1) << b for b in range(bits)
    )
    same = ((goes ^ position) == in_block // slots_per) & (
        out_block % slots_per == in_block % slots_per
    )
    ordered = jnp.dot(
        same.astype(jnp.bfloat16), hidden_grad, preferred_element_type=jnp.float32
    ).astype(jnp.bfloat16)
    back = lax.dot_general(
        ordered, w_up[0], (((1,), (1,)), ((), ())), preferred_element_type=jnp.float32
    ).astype(jnp.bfloat16)

    back, hidden_grad = hold(back, hidden_grad)
    term_up = lax.dot_general(
        hidden_grad, saved_in[0, 0], (((0,), (0,)), ((), ())), preferred_element_type=jnp.float32
    ).astype(jnp.bfloat16)
    buffer = back.reshape(1, count, slots_per, quarter)
    for level in range(levels):
        middle = buffer.shape[1] // 2
        got = partner(buffer[:, middle:], "expert", level)
        buffer = jnp.concatenate([buffer[:, :middle], got], axis=0)
        if level == 0:
            buffer, term_up = hold(buffer, term_up)
            up_pieces = scatter_along_z(term_up)
            buffer, grads_after = hold(buffer, grads_after)
    kept = behind(buffer[:, 0], 0)
    got = behind(buffer[:, 1], split)
    sums = [add_pieces(down_pieces), add_pieces(up_pieces)]
    crossed = across_x(leaving_x(sums))
    total = combine(position & (split - 1), grads_after, place_after, kept, got)
    down, up = staying_x(sums, crossed)
    return (total[None], up[None], down[None])


def solution(mesh):
    in_specs = (
        P("phase", ("dp", "expert"), None),
        P("phase", ("dp", "expert"), None),
        P("phase", ("dp", "expert"), None),
        P("phase", "dp", None, "expert"),
        P("phase", "dp", "expert", None, None),
        P("phase", "expert", None),
        P("phase", None, "expert"),
    )
    out_specs = (
        P("phase", ("dp", "expert"), None),
        P("phase", "dp", "expert"),
        P("phase", "dp", "expert"),
    )
    return jax.shard_map(body, mesh=mesh, in_specs=in_specs, out_specs=out_specs, check_vma=False)
```

```python
import jax
import jax.numpy as jnp
from jax import lax
from jax.experimental import pallas as pl
from jax.experimental.pallas import tpu as pltpu
from jax.sharding import PartitionSpec as P


def gelu_parts(pre):
    value = pre.astype(jnp.float32)
    cdf = 0.5 * (1.0 + lax.erf(value * 0.7071067811865476))
    dens = jnp.exp(-0.5 * value * value) * 0.3989422804014327
    return (value * cdf, cdf + value * dens)


def exchange(x, axis, groups=None):
    return lax.all_to_all(x, axis, 0, 0, tiled=True, axis_index_groups=groups)


def to_previous(x):
    peers = lax.axis_size("phase")
    return lax.ppermute(x, "phase", [(i, i - 1) for i in range(1, peers)])


def partner(block, axis, bit):
    count = lax.axis_size(axis)
    return lax.ppermute(block, axis, [(i, i ^ (1 << bit)) for i in range(count)])


def hold(*values):
    return lax.optimization_barrier(values)


def scatter_along_z(term):
    count = lax.axis_size("dp")
    near = count // 2
    groups = [[h * near + z for z in range(near)] for h in range(2)]
    return exchange(term, "dp", groups)


def order_for_z(term):
    count = lax.axis_size("dp")
    near = count // 2
    hid, quarter = term.shape
    ordered = term.reshape(2, near, hid // count, quarter).transpose(1, 0, 2, 3)
    return ordered.reshape(hid, quarter)


def add_pieces(pieces):
    near = lax.axis_size("dp") // 2
    hid, quarter = pieces.shape
    pieces = pieces.reshape(near, 2, hid // (2 * near), quarter)
    return jnp.sum(pieces.astype(jnp.float32), axis=0)


def leaving_x(sums):
    side = lax.axis_index("dp") // (lax.axis_size("dp") // 2)
    return jnp.stack([jnp.where(side == 1, s[0], s[1]).astype(jnp.bfloat16) for s in sums])


def across_x(away):
    count = lax.axis_size("dp")
    return lax.ppermute(away, "dp", [(i, (i + count // 2) % count) for i in range(count)])


def staying_x(sums, got):
    side = lax.axis_index("dp") // (lax.axis_size("dp") // 2)
    return [
        (jnp.where(side == 1, s[1], s[0]) + got[i].astype(jnp.float32)).astype(jnp.bfloat16)
        for i, s in enumerate(sums)
    ]


def split_by(mine, lower, upper):
    keep = jnp.where(mine == 1, upper, lower)
    away = jnp.where(mine == 1, lower, upper)
    return keep, away


def behind(block, flip):
    sections = lax.axis_size("phase")
    count = lax.axis_size("expert")
    pairs = [
        (s * count + i, (s - 1) * count + (i ^ flip)) for s in range(1, sections) for i in range(count)
    ]
    return lax.ppermute(block, ("phase", "expert"), pairs)


def combine_kernel(spot, grads, place, kept, got, out):
    quarter = kept.shape[2]
    odd = spot[0] & 1
    for c in range(2):
        columns = slice(c * quarter, (c + 1) * quarter)
        rows = jnp.concatenate([kept[c ^ odd], got[c ^ odd]], axis=0)
        added = jnp.dot(place[...], rows, preferred_element_type=jnp.float32)
        out[:, columns] = (grads[:, columns].astype(jnp.float32) + added).astype(out.dtype)


def combine(spot, grads, place, kept, got):
    tokens, width = grads.shape
    split, slots_per, quarter = kept.shape
    wide = pl.BlockSpec((tokens, 2 * quarter), lambda i, spot: (0, i ^ (spot[0] >> 1)))
    pair = pl.BlockSpec((2, slots_per, quarter), lambda i, spot: (i, 0, 0))
    return pl.pallas_call(
        combine_kernel,
        grid_spec=pltpu.PrefetchScalarGridSpec(
            num_scalar_prefetch=1,
            grid=(split // 2,),
            in_specs=[wide, pl.BlockSpec(place.shape, lambda i, spot: (0, 0)), pair, pair],
            out_specs=wide,
        ),
        out_shape=jax.ShapeDtypeStruct(grads.shape, grads.dtype),
        cost_estimate=pl.CostEstimate(
            flops=4 * tokens * slots_per * width,
            bytes_accessed=4 * tokens * width + 4 * slots_per * width,
            transcendentals=0,
        ),
        name="combine",
    )(spot.astype(jnp.int32).reshape(1), grads, place, kept, got)


def body(grad_out, routes, gates, saved_in, saved_pre, w_up, w_down):
    count = lax.axis_size("expert")
    position = lax.axis_index("expert")
    grads = grad_out[0]
    chosen = routes[0]
    weights = gates[0]
    tokens, width = grads.shape
    quarter = w_up.shape[1]
    split = width // quarter
    experts = count // split
    slots_per = saved_in.shape[2] // count
    all_slots = experts * slots_per
    levels = split.bit_length() - 1
    rows_all = count * slots_per

    expert_ids = jnp.arange(experts, dtype=jnp.int32)[:, None]
    slot_ids = jnp.arange(slots_per, dtype=jnp.int32)[None, :, None]
    names = chosen.T[:, None, :] == expert_ids[None]
    named = jnp.any(names, axis=0)
    token_ids = jnp.arange(tokens, dtype=jnp.int32)
    earlier = (token_ids[:, None] < token_ids[None, :]).astype(jnp.bfloat16)
    slot = jnp.dot(
        named.astype(jnp.bfloat16), earlier, preferred_element_type=jnp.float32
    ).astype(jnp.int32)
    hit = named[:, None, :] & (slot[:, None, :] == slot_ids)
    place = hit.astype(jnp.bfloat16).reshape(all_slots, tokens)
    pair_gate = jnp.sum(jnp.where(names, weights.T[:, None, :], 0.0), axis=0)
    gate = jnp.sum(jnp.where(hit, pair_gate[:, None, :], 0.0), axis=2).reshape(all_slots, 1)
    picked = jnp.dot(place, grads, preferred_element_type=jnp.float32)
    packed = (gate * picked).astype(jnp.bfloat16)
    outgoing = (
        packed.reshape(experts, slots_per, split, quarter)
        .transpose(0, 2, 1, 3)
        .reshape(count * slots_per, quarter)
    )
    swapped = place.reshape(experts, slots_per, tokens)[::-1].reshape(all_slots, tokens)
    place_after = to_previous(jnp.where(position >> levels == 1, swapped, place).T)
    rows = exchange(outgoing, "expert")
    rows, place_after = hold(rows, place_after)

    partial_value = lax.dot_general(
        rows, w_down[0], (((1,), (1,)), ((), ())), preferred_element_type=jnp.float32
    )
    pre = saved_pre[0, 0, 0]
    act, slope = gelu_parts(pre)
    act = act.astype(jnp.bfloat16)
    term_down = lax.dot_general(
        act, rows, (((0,), (0,)), ((), ())), preferred_element_type=jnp.float32
    ).astype(jnp.bfloat16)

    core = position & 1
    half = rows_all // 2
    keep, away = split_by(core, partial_value[:half], partial_value[half:])
    value = keep + partner(away.astype(jnp.bfloat16), "expert", 0).astype(jnp.float32)
    for level in range(1, levels):
        value = value + partner(value.astype(jnp.bfloat16), "expert", level).astype(jnp.float32)
        if level == 1:
            value, term_down = hold(value, term_down)
            down_pieces = scatter_along_z(order_for_z(term_down))
    own_slope = jnp.where(core == 1, slope[half:], slope[:half])
    own_grad = (value * own_slope).astype(jnp.bfloat16)
    other_grad = partner(own_grad, "expert", 0)
    hidden_grad = jnp.concatenate(
        [jnp.where(core == 1, other_grad, own_grad), jnp.where(core == 1, own_grad, other_grad)],
        axis=0,
    )
    grads_after = to_previous(grads)

    out_block = jnp.arange(rows_all, dtype=jnp.int32)[:, None]
    in_block = jnp.arange(rows_all, dtype=jnp.int32)[None, :]
    bits = levels + 1
    goes = sum(
        (out_block // slots_per >> (bits - 1 - b) & 1) << b for b in range(bits)
    )
    same = ((goes ^ position) == in_block // slots_per) & (
        out_block % slots_per == in_block % slots_per
    )
    ordered = jnp.dot(
        same.astype(jnp.bfloat16), hidden_grad, preferred_element_type=jnp.float32
    ).astype(jnp.bfloat16)
    back = lax.dot_general(
        ordered, w_up[0], (((1,), (1,)), ((), ())), preferred_element_type=jnp.float32
    ).astype(jnp.bfloat16)

    back, hidden_grad = hold(back, hidden_grad)
    term_up = lax.dot_general(
        hidden_grad, saved_in[0, 0], (((0,), (0,)), ((), ())), preferred_element_type=jnp.float32
    ).astype(jnp.bfloat16)
    term_up = order_for_z(term_up)
    buffer = back.reshape(1, count, slots_per, quarter)
    for level in range(levels):
        middle = buffer.shape[1] // 2
        got = partner(buffer[:, middle:], "expert", level)
        buffer = jnp.concatenate([buffer[:, :middle], got], axis=0)
        if level == 1:
            buffer, grads_after, down_pieces, term_up = hold(
                buffer, grads_after, down_pieces, term_up
            )
            up_pieces = scatter_along_z(term_up)
    kept = behind(buffer[:, 0], 0)
    got = behind(buffer[:, 1], split)
    sums = [add_pieces(down_pieces), add_pieces(up_pieces)]
    crossed = across_x(leaving_x(sums))
    total = combine(position & (split - 1), grads_after, place_after, kept, got)
    down, up = staying_x(sums, crossed)
    return (total[None], up[None], down[None])


def solution(mesh):
    in_specs = (
        P("phase", ("dp", "expert"), None),
        P("phase", ("dp", "expert"), None),
        P("phase", ("dp", "expert"), None),
        P("phase", "dp", None, "expert"),
        P("phase", "dp", "expert", None, None),
        P("phase", "expert", None),
        P("phase", None, "expert"),
    )
    out_specs = (
        P("phase", ("dp", "expert"), None),
        P("phase", "dp", "expert"),
        P("phase", "dp", "expert"),
    )
    return jax.shard_map(body, mesh=mesh, in_specs=in_specs, out_specs=out_specs, check_vma=False)
```
